32 devices in a mesh: parts: 2 (over y), blk: 4 (over z), grp: 2 (over x), fld: 2 (over core).
Axes of the slice: x: 2, y: 2, z: 4, core: 2. Of those that a mesh axis runs over, the one named last changes fastest.
Arguments:
- coords: float32 [32, 2, 2, 128], P(('parts', 'blk'), 'grp'), parts along dimension 0, may hold values from 0 to 1
- fields: float32 [32, 2, 64, 128], P(('parts', 'blk'), 'grp', 'fld'), parts along dimension 0, may hold values from -6 to 6
- neighbours: int32 [32, 2, 4], P(('parts', 'blk'), 'grp'), parts along dimension 0, may hold values from -1 to 29, as said below
Outputs:
- whitened: float32 [32, 2, 64, 128], P(('parts', 'blk'), 'grp', 'fld'), parts along dimension 0
- precision_product: float32 [32, 2, 64, 128], P(('parts', 'blk'), 'grp', 'fld'), parts along dimension 0
The draws below stay inside these ranges and needn't reach their ends.
There are 2 independent parts, one for each index of `parts`. The reference program is written for one: setup_inputs(seed, part) draws one part's arguments, and reference() takes and returns one part's arrays. A program takes and returns all parts, laid end to end along the dimension named above; each array names one. Nothing has to cross between parts.
Inputs may be any that keep to these rules, and one draw needn't show every extreme that they name: `neighbours`: each entry is -1 or the flat id j * 2 + h of a block with i - 8 <= j <= i - 1 and |h - g| <= 1, where (i, g) is the listing block; the ids of one list differ.
All inputs are finite; a program needn't handle non-finite values.
Results may differ from the reference program's by a relative error of at most 0.0003.
Values sent between devices are 32-bit elements; how exact they have to be, the bound alone decides.
A program may use at most 64 MiB of HBM per device.

```python
import jax
import jax.numpy as jnp
from jax import lax

B = 128
CONDITION_SLOTS = 4
F = 64
WINDOW = 8
ORDER_PLACES = 16
SPATIAL_GROUPS = 2


def draw_neighbours(key, part):
    slot_codes = 3 * WINDOW
    first = jax.random.fold_in(key, 11)
    second_block = jax.random.fold_in(key, 23)
    distance_scores = jax.random.randint(first, (ORDER_PLACES, SPATIAL_GROUPS, slot_codes), 0, 2 ** 20) * slot_codes + jnp.arange(slot_codes, dtype=jnp.int32)
    order_pos = jnp.arange(ORDER_PLACES, dtype=jnp.int32)[:, None, None]
    group_pos = jnp.arange(SPATIAL_GROUPS, dtype=jnp.int32)[None, :, None]
    code_pos = jnp.arange(slot_codes, dtype=jnp.int32)[None, None, :]
    forced = (order_pos == ORDER_PLACES - 1) & (group_pos == SPATIAL_GROUPS - 1) & (code_pos == 1)
    distance_scores = distance_scores + jnp.where(forced, 2 ** 30, 0).astype(jnp.int32)
    chosen_blocks = lax.top_k(distance_scores, CONDITION_SLOTS)[0] % slot_codes
    back = chosen_blocks // 3 + 1
    side = chosen_blocks % 3 - 1
    earlier = order_pos - back
    group_of = group_pos + side
    neighbour_count = jax.random.randint(second_block, (ORDER_PLACES, SPATIAL_GROUPS, 1), 1, CONDITION_SLOTS + 1)
    slot_position = jnp.arange(CONDITION_SLOTS, dtype=jnp.int32)[None, None, :]
    valid = (earlier >= 0) & (group_of >= 0) & (group_of < SPATIAL_GROUPS) & (slot_position < neighbour_count)
    return jnp.where(valid, earlier * SPATIAL_GROUPS + group_of, -1).astype(jnp.int32)


def level_of(own_key, extent, shards, least, top_value):
    factor_of, own = 1.0, jax.random.fold_in(own_key, 6)
    for dim, blocks in shards:
        heights = jnp.exp(jax.random.uniform(jax.random.fold_in(own, dim), (blocks,), jnp.float32, least / len(shards), top_value / len(shards)))
        factor_of = factor_of * jnp.repeat(heights, extent[dim] // blocks).reshape([-1 if axis == dim else 1 for axis in range(len(extent))])
    return factor_of


def scatter_about(rng, dims, scale, reach, shards=(), kind=jnp.bfloat16):
    loudness = level_of(rng, dims, shards, -0.22, 0.18) if shards else 1.0
    drawn = jax.random.normal(rng, dims, jnp.float32) * scale * loudness
    return jnp.minimum(jnp.maximum(drawn, -reach), reach).astype(kind)


def setup_inputs(seed: int = 0, part: int = 0) -> dict:
    splits = jax.random.split(jax.random.key(seed), 4)
    part_keys = jax.random.split(jax.random.fold_in(splits[3], part), 4)
    return {
        "coords": jnp.clip(1.0 * jax.random.uniform(part_keys[0], (ORDER_PLACES, SPATIAL_GROUPS, 2, B), jnp.float32) ** level_of(part_keys[0], (ORDER_PLACES, SPATIAL_GROUPS, 2, B), ((0, 4), (1, 2)), -0.2, 0.2), 0.0, 1.0),
        "fields": scatter_about(part_keys[1], (ORDER_PLACES, SPATIAL_GROUPS, F, B), 1.0, 6.0, ((0, 4), (1, 2), (2, 2)), jnp.float32),
        "neighbours": draw_neighbours(jax.random.fold_in(jax.random.fold_in(splits[3], part), 71), part),
    }


ELL = 0.3
NUGGET = 0.25

def one_block(pts, vals, mask):
    count = pts.shape[0] * pts.shape[2]
    points = jnp.transpose(pts, (0, 2, 1)).reshape(count, 2)
    mpts = jnp.repeat(mask, pts.shape[2])
    delta_x = points[:, 0][:, None] - points[:, 0][None, :]
    delta_y = points[:, 1][:, None] - points[:, 1][None, :]
    scaled = jnp.sqrt(3.0) * jnp.sqrt(delta_x * delta_x + delta_y * delta_y) / ELL
    kernel = (1.0 + scaled) * jnp.exp(-scaled)
    cov = mpts[:, None] * mpts[None, :] * kernel + jnp.diag(NUGGET * mpts + 1.0 - mpts)
    factor = jnp.linalg.cholesky(cov)
    values = jnp.transpose(vals, (0, 2, 1)).reshape(count, vals.shape[1]) * mpts[:, None]
    solved = jax.scipy.linalg.solve_triangular(factor, values, lower=True)
    mine = solved[count - pts.shape[2]:]
    padded = jnp.concatenate([jnp.zeros((count - pts.shape[2], vals.shape[1]), jnp.float32), mine], axis=0)
    back = jax.scipy.linalg.solve_triangular(factor, padded, lower=True, trans='T') * mpts[:, None]
    back = jnp.transpose(back.reshape(pts.shape[0], pts.shape[2], vals.shape[1]), (0, 2, 1))
    return (mine.T, back)

def reference(coords, fields, neighbours):
    total_count = ORDER_PLACES * SPATIAL_GROUPS
    flat_coords = coords.reshape(total_count, 2, B)
    flat_fields = fields.reshape(total_count, F, B)
    neighbour_lists = neighbours.reshape(total_count, CONDITION_SLOTS)
    own_ids = jnp.arange(total_count, dtype=jnp.int32)
    slots = jnp.concatenate([neighbour_lists, own_ids[:, None]], axis=1)
    masks = (slots >= 0).astype(jnp.float32)
    safe = jnp.where(slots >= 0, slots, own_ids[:, None]).astype(jnp.int32)

    def visit(index, carry):
        whitened, product = carry
        rows = safe[index]
        white_block, back = one_block(flat_coords[rows], flat_fields[rows], masks[index])
        whitened = whitened.at[index].set(white_block)
        product = product.at[rows].add(back)
        return (whitened, product)
    start = (jnp.zeros((total_count, F, B), jnp.float32), jnp.zeros((total_count, F, B), jnp.float32))
    whitened, product = lax.fori_loop(0, total_count, visit, start)
    return (whitened.reshape(ORDER_PLACES, SPATIAL_GROUPS, F, B), product.reshape(ORDER_PLACES, SPATIAL_GROUPS, F, B))
```

```python
import functools

import jax
import jax.numpy as jnp
from jax import lax
from jax.experimental import pallas as pl
from jax.experimental.pallas import tpu as pltpu
from jax.sharding import PartitionSpec as P

ELL = 0.3
NUGGET = 0.25
ROWS = 8
HIGHEST = lax.Precision.HIGHEST


def shifted(block, axis, distance):
    devices = range(lax.axis_size(axis))
    route = [(i - distance, i) for i in devices if i - distance in devices]
    return lax.ppermute(block, axis, route)


def dot(a, b, dims):
    return lax.dot_general(
        a, b, (dims, ((), ())), precision=HIGHEST, preferred_element_type=jnp.float32
    )


def mul(a, b):
    return dot(a, b, ((1,), (0,)))


def mul_tn(a, b):
    return dot(a, b, ((0,), (0,)))


def mul_nt(a, b):
    return dot(a, b, ((1,), (1,)))


def across_lanes(x, lane):
    return jnp.broadcast_to(x[:, lane : lane + 1], x.shape[:1] + (128,))


def across_rows(x, row):
    return jnp.broadcast_to(x[row : row + 1, :], x.shape)


def inverse_factors(mats):
    n = mats[0].shape[0]
    panels = n // ROWS
    row = lax.broadcasted_iota(jnp.int32, (ROWS, n), 0)
    lane = lax.broadcasted_iota(jnp.int32, (ROWS, n), 1)
    count = len(mats)
    s = [[m[ROWS * i : ROWS * (i + 1)] for i in range(panels)] for m in mats]
    q = [
        [jnp.where(lane == row + ROWS * i, 1.0, 0.0).astype(jnp.float32) for i in range(panels)]
        for _ in mats
    ]
    for p in range(panels):
        top = [s[c][p] for c in range(count)]
        inv = [q[c][p] for c in range(count)]
        cols = [[across_lanes(top[c], ROWS * p + j) for j in range(ROWS)] for c in range(count)]
        scale = [jnp.zeros((ROWS, n), jnp.float32) for _ in mats]
        for k in range(ROWS):
            for c in range(count):
                pivot = across_rows(cols[c][k], k)
                scale[c] = jnp.where(row == k, pivot, scale[c])
                if k == ROWS - 1:
                    continue
                m = jnp.where(row > k, cols[c][k] * (1.0 / pivot), 0.0)
                for j in range(k + 1, ROWS):
                    cols[c][j] = cols[c][j] - m * across_rows(cols[c][j], k)
                top[c] = top[c] - m * across_rows(top[c], k)
                inv[c] = inv[c] - m * across_rows(inv[c], k)
        for c in range(count):
            root = lax.rsqrt(scale[c])
            r = top[c] * root
            w = inv[c] * root
            q[c][p] = w
            if p + 1 == panels:
                continue
            rt = r.T
            rk = [across_rows(r, k) for k in range(ROWS)]
            wk = [across_rows(w, k) for k in range(ROWS)]
            for i in range(p + 1, panels):
                part = rt[ROWS * i : ROWS * (i + 1)]
                for k in range(ROWS):
                    coef = across_lanes(part, k)
                    s[c][i] = s[c][i] - coef * rk[k]
                    q[c][i] = q[c][i] - coef * wk[k]
    return [jnp.concatenate(q[c], axis=0) for c in range(count)]


def factor_kernel(slots_ref, masks_ref, window_ref, g_ref, s_ref, w_ref, xc_ref):
    half, width = g_ref.shape[0], g_ref.shape[1]
    n = g_ref.shape[2]
    both = range(half)
    for c in both:
        for t in range(width):
            pts = window_ref[slots_ref[c, t]]
            for d in range(2):
                xc_ref[c, t, d] = jnp.broadcast_to(pts[d : d + 1], (n, n)).T
    eye = lax.broadcasted_iota(jnp.int32, (n, n), 0) == lax.broadcasted_iota(
        jnp.int32, (n, n), 1
    )
    factor = 3.0 / (ELL * ELL)
    for c in both:
        for u in range(width):
            pts = window_ref[slots_ref[c, u]]
            for t in range(u + 1):
                dx = xc_ref[c, t, 0] - pts[0:1]
                dy = xc_ref[c, t, 1] - pts[1:2]
                r2 = (dx * dx + dy * dy) * factor
                scaled = r2 * lax.rsqrt(jnp.maximum(r2, 1e-30))
                value = (1.0 + scaled) * jnp.exp(-scaled)
                value = value * (masks_ref[c, t] * masks_ref[c, u])
                if t == u:
                    m = masks_ref[c, t]
                    value = value + jnp.where(eye, NUGGET * m + 1.0 - m, 0.0)
                s_ref[c, t, u] = value

    def step(t, carry):
        w = inverse_factors([s_ref[c, t, t] for c in both])
        for c in both:
            w_ref[c, t] = w[c]
        for tv in range(width - 1):

            @pl.when(t == tv)
            def _():
                b = [[None] * width for _ in both]
                for u in range(tv + 1, width):
                    for c in both:
                        b[c][u] = mul(w_ref[c, tv], s_ref[c, tv, u])
                        s_ref[c, tv, u] = b[c][u]
                for u in range(tv + 1, width):
                    for x in range(u, width):
                        for c in both:
                            s_ref[c, u, x] = s_ref[c, u, x] - mul_tn(b[c][u], b[c][x])

        return carry

    lax.fori_loop(0, width, step, 0)
    for c in both:
        g_ref[c, width - 1] = w_ref[c, width - 1]
    for t in reversed(range(width - 1)):
        for c in both:
            total = mul_nt(g_ref[c, width - 1], s_ref[c, t, width - 1])
            for u in range(t + 1, width - 1):
                total = total + mul_nt(g_ref[c, u], s_ref[c, t, u])
            g_ref[c, t] = -mul(total, w_ref[c, t])


def apply_kernel(slots_ref, first_ref, mine_ref, other_ref, fields_ref, white_ref, terms_ref):
    half, width = mine_ref.shape[0], mine_ref.shape[1]
    terms_ref[...] = jnp.zeros_like(terms_ref)
    for source, start in ((mine_ref, first_ref[0]), (other_ref, half - first_ref[0])):
        for i in range(half):
            block = start + i
            total = None
            for t in range(width):
                part = mul_nt(fields_ref[slots_ref[block, t]], source[i, t])
                total = part if total is None else total + part
            white_ref[block] = total
            for t in range(width):
                cell = slots_ref[block, t]
                terms_ref[cell] = terms_ref[cell] + mul(total, source[i, t])


def padded(cells):
    return [shifted(cells, "grp", 1), cells, shifted(cells, "grp", -1)]


def window_of(cells):
    wide = jnp.stack(padded(cells[:, 0]), axis=1)
    return jnp.concatenate(
        [shifted(wide, "blk", 2), shifted(wide, "blk", 1), wide], axis=0
    ).reshape((9 * cells.shape[0],) + cells.shape[2:])


def per_device(coords, fields, neighbours):
    per = coords.shape[0]
    local_fields = fields.shape[2]
    n = coords.shape[3]
    groups = lax.axis_size("grp")
    blk_pos = lax.axis_index("blk")
    grp_pos = lax.axis_index("grp")
    coords_window = window_of(coords)
    lists = neighbours.reshape(per, neighbours.shape[2])
    earlier = lists // groups - (blk_pos - 2) * per
    beside = lists % groups - grp_pos + 1
    own_slot = ((2 * per + jnp.arange(per, dtype=jnp.int32)) * 3 + 1)[:, None]
    slots = jnp.concatenate([jnp.where(lists >= 0, earlier * 3 + beside, own_slot), own_slot], axis=1)
    masks = jnp.concatenate(
        [(lists >= 0).astype(jnp.float32), jnp.ones((per, 1), jnp.float32)], axis=1
    )
    width = slots.shape[1]
    half = per // lax.axis_size("fld")
    first = lax.axis_index("fld") * half
    my_slots = lax.dynamic_slice_in_dim(slots, first, half, 0)
    my_masks = lax.dynamic_slice_in_dim(masks, first, half, 0)
    smem = pl.BlockSpec(memory_space=pltpu.SMEM)
    vmem = pl.BlockSpec(memory_space=pltpu.VMEM)
    mine = pl.pallas_call(
        factor_kernel,
        out_shape=jax.ShapeDtypeStruct((half, width, n, n), jnp.float32),
        in_specs=[smem, smem, vmem],
        out_specs=vmem,
        scratch_shapes=[
            pltpu.VMEM((half, width, width, n, n), jnp.float32),
            pltpu.VMEM((half, width, n, n), jnp.float32),
            pltpu.VMEM((half, width, 2, n, n), jnp.float32),
        ],
        cost_estimate=pl.CostEstimate(
            flops=60_000_000_000, bytes_accessed=1_000_000, transcendentals=1_000_000
        ),
        compiler_params=pltpu.CompilerParams(vmem_limit_bytes=32 * 1024 * 1024),
        name="factor",
    )(my_slots, my_masks, coords_window)
    fields_window = window_of(fields)
    other = lax.ppermute(mine, "fld", [(0, 1), (1, 0)])
    whitened, terms = pl.pallas_call(
        apply_kernel,
        out_shape=(
            jax.ShapeDtypeStruct((per, local_fields, n), jnp.float32),
            jax.ShapeDtypeStruct((9 * per, local_fields, n), jnp.float32),
        ),
        in_specs=[smem, smem, vmem, vmem, vmem],
        out_specs=(vmem, vmem),
        compiler_params=pltpu.CompilerParams(vmem_limit_bytes=32 * 1024 * 1024),
        name="apply",
    )(slots, first.reshape(1), mine, other, fields_window)
    terms = terms.reshape(3, per, 3, local_fields, n)
    total = terms[2]
    for distance in (1, 2):
        total = total + shifted(terms[2 - distance], "blk", -distance)
    product = total[:, 1]
    for column, offset in ((0, -1), (2, 1)):
        product = product + shifted(total[:, column], "grp", offset)
    return (whitened[:, None], product[:, None])


def solution(mesh):
    return jax.shard_map(
        per_device,
        mesh=mesh,
        in_specs=(
            P(("parts", "blk"), "grp", None, None),
            P(("parts", "blk"), "grp", "fld", None),
            P(("parts", "blk"), "grp", None),
        ),
        out_specs=(
            P(("parts", "blk"), "grp", "fld", None),
            P(("parts", "blk"), "grp", "fld", None),
        ),
        check_vma=False,
    )
```

```python
import functools

import jax
import jax.numpy as jnp
from jax import lax
from jax.experimental import pallas as pl
from jax.experimental.pallas import tpu as pltpu
from jax.sharding import PartitionSpec as P

ELL = 0.3
NUGGET = 0.25
ROWS = 8
HIGHEST = lax.Precision.HIGHEST


def dot(a, b, dims):
    return lax.dot_general(
        a, b, (dims, ((), ())), precision=HIGHEST, preferred_element_type=jnp.float32
    )


def mul(a, b):
    return dot(a, b, ((1,), (0,)))


def mul_tn(a, b):
    return dot(a, b, ((0,), (0,)))


def mul_nt(a, b):
    return dot(a, b, ((1,), (1,)))


def across_lanes(x, lane):
    return jnp.broadcast_to(x[:, lane : lane + 1], x.shape[:1] + (128,))


def across_rows(x, row):
    return jnp.broadcast_to(x[row : row + 1, :], x.shape)


def inverse_factors(mats):
    n = mats[0].shape[0]
    panels = n // ROWS
    row = lax.broadcasted_iota(jnp.int32, (ROWS, n), 0)
    lane = lax.broadcasted_iota(jnp.int32, (ROWS, n), 1)
    count = len(mats)
    s = [[m[ROWS * i : ROWS * (i + 1)] for i in range(panels)] for m in mats]
    q = [
        [jnp.where(lane == row + ROWS * i, 1.0, 0.0).astype(jnp.float32) for i in range(panels)]
        for _ in mats
    ]
    for p in range(panels):
        top = [s[c][p] for c in range(count)]
        inv = [q[c][p] for c in range(count)]
        cols = [[across_lanes(top[c], ROWS * p + j) for j in range(ROWS)] for c in range(count)]
        scale = [jnp.zeros((ROWS, n), jnp.float32) for _ in mats]
        for k in range(ROWS):
            for c in range(count):
                pivot = across_rows(cols[c][k], k)
                scale[c] = jnp.where(row == k, pivot, scale[c])
                if k == ROWS - 1:
                    continue
                m = jnp.where(row > k, cols[c][k] * (1.0 / pivot), 0.0)
                for j in range(k + 1, ROWS):
                    cols[c][j] = cols[c][j] - m * across_rows(cols[c][j], k)
                top[c] = top[c] - m * across_rows(top[c], k)
                inv[c] = inv[c] - m * across_rows(inv[c], k)
        for c in range(count):
            root = lax.rsqrt(scale[c])
            r = top[c] * root
            w = inv[c] * root
            q[c][p] = w
            if p + 1 == panels:
                continue
            rt = r.T
            rk = [across_rows(r, k) for k in range(ROWS)]
            wk = [across_rows(w, k) for k in range(ROWS)]
            for i in range(p + 1, panels):
                part = rt[ROWS * i : ROWS * (i + 1)]
                for k in range(ROWS):
                    coef = across_lanes(part, k)
                    s[c][i] = s[c][i] - coef * rk[k]
                    q[c][i] = q[c][i] - coef * wk[k]
    return [jnp.concatenate(q[c], axis=0) for c in range(count)]


def window_kernel(
    slots_ref,
    masks_ref,
    coords_ref,
    fields_ref,
    white_ref,
    product_ref,
    coords_win,
    fields_win,
    s_ref,
    w_ref,
    xc_ref,
    mine_ref,
    other_ref,
    v_ref,
    terms_ref,
    back_ref,
    coords_send,
    coords_recv,
    fields_send,
    fields_recv,
    swap_send,
    swap_recv,
    back_send,
    back_recv,
):
    width, half, n = mine_ref.shape[0], mine_ref.shape[1], mine_ref.shape[2]
    per = fields_ref.shape[0]
    both = range(half)
    blk, grp, fld = (lax.axis_index(a) for a in ("blk", "grp", "fld"))
    blks, grps = lax.axis_size("blk"), lax.axis_size("grp")
    first = fld * half
    partner = {"fld": 1 - fld}
    routes = [(z, x) for z in (2, 1, 0) for x in (-1, 0, 1) if (z, x) != (0, 0)]

    def there(z, x):
        return (blk + z >= 0) & (blk + z < blks) & (grp + x >= 0) & (grp + x < grps)

    def place(z, x):
        return {"blk": blk + z, "grp": grp + x}

    coords_win[...] = jnp.zeros_like(coords_win)
    fields_win[...] = jnp.zeros_like(fields_win)
    barrier = pltpu.get_barrier_semaphore()
    pl.semaphore_signal(barrier, inc=1, device_id=partner, device_id_type=pl.DeviceIdType.MESH)
    around = jnp.int32(1)
    for z in range(-2, 3):
        for x in (-1, 0, 1):
            if (z, x) == (0, 0):
                continue

            @pl.when(there(z, x))
            def _():
                pl.semaphore_signal(
                    barrier, inc=1, device_id=place(z, x), device_id_type=pl.DeviceIdType.MESH
                )

            around = around + there(z, x).astype(jnp.int32)
    pl.semaphore_wait(barrier, around)

    def out_copy(source, window, send, recv, z, x):
        index = routes.index((z, x))
        cell = (2 - z) * 3 + 1 - x
        return pltpu.make_async_remote_copy(
            src_ref=source,
            dst_ref=window.at[pl.ds(cell * per, per)],
            send_sem=send.at[index],
            recv_sem=recv.at[index],
            device_id=place(z, x),
            device_id_type=pl.DeviceIdType.MESH,
        )

    def coords_copy(z, x):
        return out_copy(coords_ref, coords_win, coords_send, coords_recv, z, x)

    def fields_copy(z, x):
        return out_copy(fields_ref, fields_win, fields_send, fields_recv, z, x)

    def back_copy(z, x):
        index = routes.index((z, x))
        cell = (2 - z) * 3 + 1 - x
        return pltpu.make_async_remote_copy(
            src_ref=terms_ref.at[pl.ds(cell * per, per)],
            dst_ref=back_ref.at[index],
            send_sem=back_send.at[index],
            recv_sem=back_recv.at[index],
            device_id=place(-z, -x),
            device_id_type=pl.DeviceIdType.MESH,
        )

    def on(condition, act):
        @pl.when(condition)
        def _():
            act()

    for z, x in routes:
        on(there(z, x), lambda: coords_copy(z, x).start())
    for z, x in routes:
        on(there(z, x), lambda: fields_copy(z, x).start())
    own = (2 * 3 + 1) * per
    coords_win[pl.ds(own, per)] = coords_ref[...]
    fields_win[pl.ds(own, per)] = fields_ref[...]
    for z, x in routes:
        on(there(-z, -x), lambda: coords_copy(z, x).wait_recv())

    def slot(block, t):
        return slots_ref[block, t]

    for c in both:
        for t in range(width):
            pts = coords_win[slot(first + c, t)]
            for d in range(2):
                xc_ref[c, t, d] = jnp.broadcast_to(pts[d : d + 1], (n, n)).T
    eye = lax.broadcasted_iota(jnp.int32, (n, n), 0) == lax.broadcasted_iota(
        jnp.int32, (n, n), 1
    )
    factor = 3.0 / (ELL * ELL)
    for c in both:
        for u in range(width):
            pts = coords_win[slot(first + c, u)]
            mu = masks_ref[first + c, u]
            for t in range(u + 1):
                dx = xc_ref[c, t, 0] - pts[0:1]
                dy = xc_ref[c, t, 1] - pts[1:2]
                r2 = (dx * dx + dy * dy) * factor
                scaled = r2 * lax.rsqrt(jnp.maximum(r2, 1e-30))
                value = (1.0 + scaled) * jnp.exp(-scaled)
                value = value * (masks_ref[first + c, t] * mu)
                if t == u:
                    value = value + jnp.where(eye, NUGGET * mu + 1.0 - mu, 0.0)
                s_ref[c, t, u] = value

    def step(t, carry):
        w = inverse_factors([s_ref[c, t, t] for c in both])
        for c in both:
            w_ref[c, t] = w[c]
        for tv in range(width - 1):

            @pl.when(t == tv)
            def _():
                b = [[None] * width for _ in both]
                for u in range(tv + 1, width):
                    for c in both:
                        b[c][u] = mul(w_ref[c, tv], s_ref[c, tv, u])
                        s_ref[c, tv, u] = b[c][u]
                for u in range(tv + 1, width):
                    for x in range(u, width):
                        for c in both:
                            s_ref[c, u, x] = s_ref[c, u, x] - mul_tn(b[c][u], b[c][x])

        return carry

    lax.fori_loop(0, width, step, 0)

    def swap(t):
        return pltpu.make_async_remote_copy(
            src_ref=mine_ref.at[t],
            dst_ref=other_ref.at[t],
            send_sem=swap_send.at[t],
            recv_sem=swap_recv.at[t],
            device_id=partner,
            device_id_type=pl.DeviceIdType.MESH,
        )

    for t in reversed(range(width)):
        for c in both:
            if t == width - 1:
                mine_ref[t, c] = w_ref[c, t]
                continue
            total = mul_nt(mine_ref[width - 1, c], s_ref[c, t, width - 1])
            for u in range(t + 1, width - 1):
                total = total + mul_nt(mine_ref[u, c], s_ref[c, t, u])
            mine_ref[t, c] = -mul(total, w_ref[c, t])
        swap(t).start()
    for z, x in routes:
        on(there(-z, -x), lambda: fields_copy(z, x).wait_recv())

    def apply(source, start):
        for c in both:
            block = start + c
            total = None
            for t in range(width):
                part = mul_nt(fields_win[slot(block, t)], source[t, c])
                total = part if total is None else total + part
            white_ref[block] = total
            for t in range(width):
                v_ref[block, t] = mul(total, source[t, c])

    apply(mine_ref, first)
    for t in reversed(range(width)):
        swap(t).wait_recv()
    apply(other_ref, half - first)

    def gather_terms(z, x):
        cell = (2 - z) * 3 + 1 - x
        for i in range(per):
            total = None
            if (z, x) == (0, 0):
                total = v_ref[i, width - 1]
            order = (2 - z) * per + i
            for block in range(per):
                if not block <= order < block + 2 * per:
                    continue
                for t in range(width - 1):
                    v = v_ref[block, t]
                    part = jnp.where(slot(block, t) == cell * per + i, v, jnp.zeros_like(v))
                    total = part if total is None else total + part
            if total is None:
                total = jnp.zeros_like(v_ref[0, 0])
            terms_ref[cell * per + i] = total

    for z, x in routes:

        def send_terms(z=z, x=x):
            gather_terms(z, x)
            back_copy(z, x).start()

        on(there(-z, -x), send_terms)
    gather_terms(0, 0)
    product_ref[...] = terms_ref[pl.ds(own, per)]
    for index, (z, x) in enumerate(routes):

        def add_back(z=z, x=x, index=index):
            back_copy(z, x).wait_recv()
            product_ref[...] += back_ref[index]

        on(there(z, x), add_back)
    for t in range(width):
        swap(t).wait_send()
    for z, x in routes:

        def sent(z=z, x=x):
            coords_copy(z, x).wait_send()
            fields_copy(z, x).wait_send()

        on(there(z, x), sent)
        on(there(-z, -x), lambda: back_copy(z, x).wait_send())


def per_device(coords, fields, neighbours):
    per = coords.shape[0]
    local_fields = fields.shape[2]
    n = coords.shape[3]
    groups = lax.axis_size("grp")
    blk_pos = lax.axis_index("blk")
    grp_pos = lax.axis_index("grp")
    lists = neighbours.reshape(per, neighbours.shape[2])
    earlier = lists // groups - (blk_pos - 2) * per
    beside = lists % groups - grp_pos + 1
    listed = ((earlier // per) * 3 + beside) * per + earlier % per
    own_slot = (7 * per + jnp.arange(per, dtype=jnp.int32))[:, None]
    slots = jnp.concatenate([jnp.where(lists >= 0, listed, own_slot), own_slot], axis=1)
    masks = jnp.concatenate(
        [(lists >= 0).astype(jnp.float32), jnp.ones((per, 1), jnp.float32)], axis=1
    )
    width = slots.shape[1]
    half = per // lax.axis_size("fld")
    smem = pl.BlockSpec(memory_space=pltpu.SMEM)
    vmem = pl.BlockSpec(memory_space=pltpu.VMEM)
    block = (per, local_fields, n)
    dma = pltpu.SemaphoreType.DMA
    whitened, product = pl.pallas_call(
        window_kernel,
        out_shape=(jax.ShapeDtypeStruct(block, jnp.float32),) * 2,
        in_specs=[smem, smem, vmem, vmem],
        out_specs=(vmem, vmem),
        scratch_shapes=[
            pltpu.VMEM((9 * per, 2, n), jnp.float32),
            pltpu.VMEM((9 * per, local_fields, n), jnp.float32),
            pltpu.VMEM((half, width, width, n, n), jnp.float32),
            pltpu.VMEM((half, width, n, n), jnp.float32),
            pltpu.VMEM((half, width, 2, n, n), jnp.float32),
            pltpu.VMEM((width, half, n, n), jnp.float32),
            pltpu.VMEM((width, half, n, n), jnp.float32),
            pltpu.VMEM((per, width, local_fields, n), jnp.float32),
            pltpu.VMEM((9 * per, local_fields, n), jnp.float32),
            pltpu.VMEM((8,) + block, jnp.float32),
            dma((8,)),
            dma((8,)),
            dma((8,)),
            dma((8,)),
            dma((width,)),
            dma((width,)),
            dma((8,)),
            dma((8,)),
        ],
        compiler_params=pltpu.CompilerParams(
            vmem_limit_bytes=40 * 1024 * 1024, collective_id=0, has_side_effects=True
        ),
        name="window",
    )(slots, masks, coords.reshape(per, 2, n), fields.reshape(block))
    return (whitened[:, None], product[:, None])


def solution(mesh):
    return jax.shard_map(
        per_device,
        mesh=mesh,
        in_specs=(
            P(("parts", "blk"), "grp", None, None),
            P(("parts", "blk"), "grp", "fld", None),
            P(("parts", "blk"), "grp", None),
        ),
        out_specs=(
            P(("parts", "blk"), "grp", "fld", None),
            P(("parts", "blk"), "grp", "fld", None),
        ),
        check_vma=False,
    )
```

```python
import functools

import jax
import jax.numpy as jnp
from jax import lax
from jax.experimental import pallas as pl
from jax.experimental.pallas import tpu as pltpu
from jax.sharding import PartitionSpec as P

ELL = 0.3
NUGGET = 0.25
ROWS = 8
HIGHEST = lax.Precision.HIGHEST


def dot(a, b, dims):
    return lax.dot_general(
        a, b, (dims, ((), ())), precision=HIGHEST, preferred_element_type=jnp.float32
    )


def mul(a, b):
    return dot(a, b, ((1,), (0,)))


def mul_tn(a, b):
    return dot(a, b, ((0,), (0,)))


def mul_nt(a, b):
    return dot(a, b, ((1,), (1,)))


def across_lanes(x, lane):
    return jnp.broadcast_to(x[:, lane : lane + 1], x.shape[:1] + (128,))


def across_rows(x, row):
    return jnp.broadcast_to(x[row : row + 1, :], x.shape)


def inverse_factors(mats):
    n = mats[0].shape[0]
    panels = n // ROWS
    row = lax.broadcasted_iota(jnp.int32, (ROWS, n), 0)
    lane = lax.broadcasted_iota(jnp.int32, (ROWS, n), 1)
    count = len(mats)
    every = range(count)
    s = [[m[ROWS * i : ROWS * (i + 1)] for i in range(panels)] for m in mats]
    q = [
        [jnp.where(lane == row + ROWS * i, 1.0, 0.0).astype(jnp.float32) for i in range(panels)]
        for _ in mats
    ]
    leaf = 2 * ROWS
    for p in range(0, panels, 2):
        top = [[s[c][p + h] for h in range(2)] for c in every]
        inv = [[q[c][p + h] for h in range(2)] for c in every]
        cols = [
            [[across_lanes(top[c][h], ROWS * p + j) for j in range(leaf)] for h in range(2)]
            for c in every
        ]
        scale = [[None, None] for _ in mats]
        for k in range(0, leaf, 2):
            g, k0 = k // ROWS, k % ROWS
            k1 = k0 + 1
            for c in every:
                x = cols[c]
                pa = across_rows(x[g][k], k0)
                pb = across_rows(x[g][k + 1], k0)
                pc = across_rows(x[g][k + 1], k1)
                det = pa * pc - pb * pb
                over = 1.0 / det
                over_a = 1.0 / pa
                old = jnp.ones_like(pa) if scale[c][g] is None else scale[c][g]
                scale[c][g] = jnp.where(row == k0, pa, jnp.where(row == k1, det * over_a, old))
                rows_j = {
                    j: (across_rows(x[g][j], k0), across_rows(x[g][j], k1))
                    for j in range(k + 2, leaf)
                }
                top_k = (across_rows(top[c][g], k0), across_rows(top[c][g], k1))
                inv_k = (across_rows(inv[c][g], k0), across_rows(inv[c][g], k1))
                for h in range(g, 2):
                    n0 = pc * x[h][k] - pb * x[h][k + 1]
                    n1 = pa * x[h][k + 1] - pb * x[h][k]
                    if h == g:
                        n0 = jnp.where(row > k1, n0, 0.0)
                        n1 = jnp.where(row > k1, n1, 0.0)
                    m0 = n0 * over
                    m1 = n1 * over
                    if not (h == g and k1 == ROWS - 1):
                        for j in range(k + 2, leaf):
                            u0, u1 = rows_j[j]
                            if j < k + 4:
                                x[h][j] = x[h][j] - (n0 * u0 + n1 * u1) * over
                            else:
                                x[h][j] = x[h][j] - (m0 * u0 + m1 * u1)
                    if h == g:
                        m0 = jnp.where(row == k1, pb * over_a, m0)
                    top[c][h] = top[c][h] - (m0 * top_k[0] + m1 * top_k[1])
                    inv[c][h] = inv[c][h] - (m0 * inv_k[0] + m1 * inv_k[1])
        for c in every:
            roots = [lax.rsqrt(scale[c][h]) for h in range(2)]
            r = [top[c][h] * roots[h] for h in range(2)]
            w = [inv[c][h] * roots[h] for h in range(2)]
            for h in range(2):
                q[c][p + h] = w[h]
            if p + 2 == panels:
                continue
            rt = jnp.concatenate(r, axis=0).T
            rk = [across_rows(r[k // ROWS], k % ROWS) for k in range(leaf)]
            wk = [across_rows(w[k // ROWS], k % ROWS) for k in range(leaf)]
            for i in range(p + 2, panels):
                part = rt[ROWS * i : ROWS * (i + 1)]
                sums = [None, None]
                for k in range(0, leaf, 2):
                    c0, c1 = across_lanes(part, k), across_lanes(part, k + 1)
                    for index, held in enumerate((rk, wk)):
                        both = c0 * held[k] + c1 * held[k + 1]
                        sums[index] = both if sums[index] is None else sums[index] + both
                s[c][i] = s[c][i] - sums[0]
                q[c][i] = q[c][i] - sums[1]
    return [jnp.concatenate(q[c], axis=0) for c in every]


def window_kernel(
    slots_ref,
    masks_ref,
    coords_ref,
    fields_ref,
    white_ref,
    product_ref,
    coords_win,
    fields_win,
    s_ref,
    w_ref,
    xc_ref,
    mine_ref,
    other_ref,
    v_ref,
    terms_ref,
    back_ref,
    coords_send,
    coords_recv,
    fields_send,
    fields_recv,
    swap_send,
    swap_recv,
    back_send,
    back_recv,
):
    half, n = mine_ref.shape[0], mine_ref.shape[1]
    width = mine_ref.shape[2] // n
    per = fields_ref.shape[0]
    both = range(half)
    blk, grp, fld = (lax.axis_index(a) for a in ("blk", "grp", "fld"))
    blks, grps = lax.axis_size("blk"), lax.axis_size("grp")
    first = fld * half
    partner = {"fld": 1 - fld}
    routes = [(z, x) for z in (2, 1, 0) for x in (-1, 0, 1) if (z, x) != (0, 0)]

    def there(z, x):
        return (blk + z >= 0) & (blk + z < blks) & (grp + x >= 0) & (grp + x < grps)

    def place(z, x):
        return {"blk": blk + z, "grp": grp + x}

    coords_win[...] = jnp.zeros_like(coords_win)
    fields_win[...] = jnp.zeros_like(fields_win)
    barrier = pltpu.get_barrier_semaphore()
    pl.semaphore_signal(barrier, inc=1, device_id=partner, device_id_type=pl.DeviceIdType.MESH)
    around = jnp.int32(1)
    for z in range(-2, 3):
        for x in (-1, 0, 1):
            if (z, x) == (0, 0):
                continue

            @pl.when(there(z, x))
            def _():
                pl.semaphore_signal(
                    barrier, inc=1, device_id=place(z, x), device_id_type=pl.DeviceIdType.MESH
                )

            around = around + there(z, x).astype(jnp.int32)
    pl.semaphore_wait(barrier, around)

    def out_copy(source, window, send, recv, z, x):
        index = routes.index((z, x))
        cell = (2 - z) * 3 + 1 - x
        return pltpu.make_async_remote_copy(
            src_ref=source,
            dst_ref=window.at[pl.ds(cell * per, per)],
            send_sem=send.at[index],
            recv_sem=recv.at[index],
            device_id=place(z, x),
            device_id_type=pl.DeviceIdType.MESH,
        )

    def coords_copy(z, x):
        return out_copy(coords_ref, coords_win, coords_send, coords_recv, z, x)

    def fields_copy(z, x):
        return out_copy(fields_ref, fields_win, fields_send, fields_recv, z, x)

    def back_copy(z, x):
        index = routes.index((z, x))
        cell = (2 - z) * 3 + 1 - x
        return pltpu.make_async_remote_copy(
            src_ref=terms_ref.at[pl.ds(cell * per, per)],
            dst_ref=back_ref.at[index],
            send_sem=back_send.at[index],
            recv_sem=back_recv.at[index],
            device_id=place(-z, -x),
            device_id_type=pl.DeviceIdType.MESH,
        )

    def on(condition, act):
        @pl.when(condition)
        def _():
            act()

    for z, x in routes:
        on(there(z, x), lambda: coords_copy(z, x).start())
    for z, x in routes:
        on(there(z, x), lambda: fields_copy(z, x).start())
    own = (2 * 3 + 1) * per
    coords_win[pl.ds(own, per)] = coords_ref[...]
    fields_win[pl.ds(own, per)] = fields_ref[...]
    for z, x in routes:
        on(there(-z, -x), lambda: coords_copy(z, x).wait_recv())

    def slot(block, t):
        return slots_ref[block, t]

    for c in both:
        for t in range(width):
            pts = coords_win[slot(first + c, t)]
            for d in range(2):
                xc_ref[c, t, d] = jnp.broadcast_to(pts[d : d + 1], (n, n)).T
    eye = lax.broadcasted_iota(jnp.int32, (n, n), 0) == lax.broadcasted_iota(
        jnp.int32, (n, n), 1
    )
    factor = 3.0 / (ELL * ELL)
    for c in both:
        for u in range(width):
            pts = coords_win[slot(first + c, u)]
            mu = masks_ref[first + c, u]
            for t in range(u + 1):
                dx = xc_ref[c, t, 0] - pts[0:1]
                dy = xc_ref[c, t, 1] - pts[1:2]
                r2 = (dx * dx + dy * dy) * factor
                scaled = r2 * lax.rsqrt(jnp.maximum(r2, 1e-30))
                value = (1.0 + scaled) * jnp.exp(-scaled)
                value = value * (masks_ref[first + c, t] * mu)
                if t == u:
                    value = value + jnp.where(eye, NUGGET * mu + 1.0 - mu, 0.0)
                s_ref[c, t, :, u * n : (u + 1) * n] = value

    def step(t, carry):
        w = inverse_factors([s_ref[c, t, :, pl.ds(pl.multiple_of(t * n, n), n)] for c in both])
        for c in both:
            w_ref[c, t] = w[c]
        for tv in range(width - 1):

            @pl.when(t == tv)
            def _():
                b = [mul(w_ref[c, tv], s_ref[c, tv, :, (tv + 1) * n :]) for c in both]
                for c in both:
                    s_ref[c, tv, :, (tv + 1) * n :] = b[c]
                for u in range(tv + 1, width):
                    skip = (u - tv - 1) * n
                    for c in both:
                        s_ref[c, u, :, u * n :] = s_ref[c, u, :, u * n :] - mul_tn(
                            b[c][:, skip : skip + n], b[c][:, skip:]
                        )

        return carry

    lax.fori_loop(0, width, step, 0)

    def swap(t):
        piece = pl.ds(t * n, n)
        return pltpu.make_async_remote_copy(
            src_ref=mine_ref.at[:, :, piece],
            dst_ref=other_ref.at[:, :, piece],
            send_sem=swap_send.at[t],
            recv_sem=swap_recv.at[t],
            device_id=partner,
            device_id_type=pl.DeviceIdType.MESH,
        )

    for t in reversed(range(width)):
        for c in both:
            if t == width - 1:
                mine_ref[c, :, t * n :] = w_ref[c, t]
                continue
            later = (t + 1) * n
            total = mul_nt(mine_ref[c, :, later:], s_ref[c, t, :, later:])
            mine_ref[c, :, t * n : later] = -mul(total, w_ref[c, t])
        swap(t).start()
    for z, x in routes:
        on(there(-z, -x), lambda: fields_copy(z, x).wait_recv())

    def apply(source, start):
        for c in both:
            block = start + c
            values = jnp.concatenate([fields_win[slot(block, t)] for t in range(width)], axis=1)
            total = mul_nt(values, source[c])
            white_ref[block] = total
            v_ref[block] = mul(total, source[c])

    apply(mine_ref, first)
    for t in reversed(range(width)):
        swap(t).wait_recv()
    apply(other_ref, half - first)

    def gather_terms(z, x):
        cell = (2 - z) * 3 + 1 - x
        for i in range(per):
            total = None
            if (z, x) == (0, 0):
                total = v_ref[i, :, (width - 1) * n :]
            order = (2 - z) * per + i
            for block in range(per):
                if not block <= order < block + 2 * per:
                    continue
                for t in range(width - 1):
                    v = v_ref[block, :, t * n : (t + 1) * n]
                    part = jnp.where(slot(block, t) == cell * per + i, v, jnp.zeros_like(v))
                    total = part if total is None else total + part
            if total is None:
                total = jnp.zeros_like(terms_ref[0])
            terms_ref[cell * per + i] = total

    for z, x in routes:

        def send_terms(z=z, x=x):
            gather_terms(z, x)
            back_copy(z, x).start()

        on(there(-z, -x), send_terms)
    gather_terms(0, 0)
    product_ref[...] = terms_ref[pl.ds(own, per)]
    for index, (z, x) in enumerate(routes):

        def add_back(z=z, x=x, index=index):
            back_copy(z, x).wait_recv()
            product_ref[...] += back_ref[index]

        on(there(z, x), add_back)
    for t in range(width):
        swap(t).wait_send()
    for z, x in routes:

        def sent(z=z, x=x):
            coords_copy(z, x).wait_send()
            fields_copy(z, x).wait_send()

        on(there(z, x), sent)
        on(there(-z, -x), lambda: back_copy(z, x).wait_send())


def per_device(coords, fields, neighbours):
    per = coords.shape[0]
    local_fields = fields.shape[2]
    n = coords.shape[3]
    groups = lax.axis_size("grp")
    blk_pos = lax.axis_index("blk")
    grp_pos = lax.axis_index("grp")
    lists = neighbours.reshape(per, neighbours.shape[2])
    earlier = lists // groups - (blk_pos - 2) * per
    beside = lists % groups - grp_pos + 1
    listed = ((earlier // per) * 3 + beside) * per + earlier % per
    own_slot = (7 * per + jnp.arange(per, dtype=jnp.int32))[:, None]
    slots = jnp.concatenate([jnp.where(lists >= 0, listed, own_slot), own_slot], axis=1)
    masks = jnp.concatenate(
        [(lists >= 0).astype(jnp.float32), jnp.ones((per, 1), jnp.float32)], axis=1
    )
    width = slots.shape[1]
    half = per // lax.axis_size("fld")
    smem = pl.BlockSpec(memory_space=pltpu.SMEM)
    vmem = pl.BlockSpec(memory_space=pltpu.VMEM)
    block = (per, local_fields, n)
    dma = pltpu.SemaphoreType.DMA
    whitened, product = pl.pallas_call(
        window_kernel,
        out_shape=(jax.ShapeDtypeStruct(block, jnp.float32),) * 2,
        in_specs=[smem, smem, vmem, vmem],
        out_specs=(vmem, vmem),
        scratch_shapes=[
            pltpu.VMEM((9 * per, 2, n), jnp.float32),
            pltpu.VMEM((9 * per, local_fields, n), jnp.float32),
            pltpu.VMEM((half, width, n, width * n), jnp.float32),
            pltpu.VMEM((half, width, n, n), jnp.float32),
            pltpu.VMEM((half, width, 2, n, n), jnp.float32),
            pltpu.VMEM((half, n, width * n), jnp.float32),
            pltpu.VMEM((half, n, width * n), jnp.float32),
            pltpu.VMEM((per, local_fields, width * n), jnp.float32),
            pltpu.VMEM((9 * per, local_fields, n), jnp.float32),
            pltpu.VMEM((8,) + block, jnp.float32),
            dma((8,)),
            dma((8,)),
            dma((8,)),
            dma((8,)),
            dma((width,)),
            dma((width,)),
            dma((8,)),
            dma((8,)),
        ],
        compiler_params=pltpu.CompilerParams(
            vmem_limit_bytes=40 * 1024 * 1024, collective_id=0, has_side_effects=True
        ),
        name="window",
    )(slots, masks, coords.reshape(per, 2, n), fields.reshape(block))
    return (whitened[:, None], product[:, None])


def solution(mesh):
    return jax.shard_map(
        per_device,
        mesh=mesh,
        in_specs=(
            P(("parts", "blk"), "grp", None, None),
            P(("parts", "blk"), "grp", "fld", None),
            P(("parts", "blk"), "grp", None),
        ),
        out_specs=(
            P(("parts", "blk"), "grp", "fld", None),
            P(("parts", "blk"), "grp", "fld", None),
        ),
        check_vma=False,
    )
```

```python
import functools

import jax
import jax.numpy as jnp
from jax import lax
from jax.experimental import pallas as pl
from jax.experimental.pallas import tpu as pltpu
from jax.sharding import PartitionSpec as P

ELL = 0.3
NUGGET = 0.25
ROWS = 8
HIGHEST = lax.Precision.HIGHEST


def dot(a, b, dims):
    return lax.dot_general(
        a, b, (dims, ((), ())), precision=HIGHEST, preferred_element_type=jnp.float32
    )


def mul(a, b):
    return dot(a, b, ((1,), (0,)))


def mul_tn(a, b):
    return dot(a, b, ((0,), (0,)))


def mul_nt(a, b):
    return dot(a, b, ((1,), (1,)))


def across_lanes(x, lane):
    return jnp.broadcast_to(x[:, lane : lane + 1], x.shape[:1] + (128,))


def across_rows(x, row):
    return jnp.broadcast_to(x[row : row + 1, :], x.shape)


def packed_factors(pair):
    m, n = pair.shape
    panels = m // ROWS
    row = lax.broadcasted_iota(jnp.int32, (ROWS, n), 0)
    lane = lax.broadcasted_iota(jnp.int32, (ROWS, n), 1)
    left = lane < m
    s = [pair[ROWS * i : ROWS * (i + 1)] for i in range(panels)]
    q = [
        jnp.where(lane % m == row + ROWS * i, 1.0, 0.0).astype(jnp.float32) for i in range(panels)
    ]
    leaf = 2 * ROWS
    for p in range(0, panels, 2):
        top = [s[p], s[p + 1]]
        inv = [q[p], q[p + 1]]
        x = [
            [
                jnp.where(
                    left,
                    across_lanes(top[h], ROWS * p + j),
                    across_lanes(top[h], m + ROWS * p + j),
                )
                for j in range(leaf)
            ]
            for h in range(2)
        ]
        scale = [jnp.ones_like(top[0]) for _ in range(2)]
        for k in range(0, leaf, 2):
            g, k0 = k // ROWS, k % ROWS
            k1 = k0 + 1
            pa = across_rows(x[g][k], k0)
            pb = across_rows(x[g][k + 1], k0)
            pc = across_rows(x[g][k + 1], k1)
            det = pa * pc - pb * pb
            over = 1.0 / det
            over_a = 1.0 / pa
            scale[g] = jnp.where(row == k0, pa, jnp.where(row == k1, det * over_a, scale[g]))
            rows_j = {
                j: (across_rows(x[g][j], k0), across_rows(x[g][j], k1))
                for j in range(k + 2, leaf)
            }
            top_k = (across_rows(top[g], k0), across_rows(top[g], k1))
            inv_k = (across_rows(inv[g], k0), across_rows(inv[g], k1))
            for h in range(g, 2):
                n0 = pc * x[h][k] - pb * x[h][k + 1]
                n1 = pa * x[h][k + 1] - pb * x[h][k]
                if h == g:
                    n0 = jnp.where(row > k1, n0, 0.0)
                    n1 = jnp.where(row > k1, n1, 0.0)
                m0 = n0 * over
                m1 = n1 * over
                if not (h == g and k1 == ROWS - 1):
                    for j in range(k + 2, leaf):
                        u0, u1 = rows_j[j]
                        if j < k + 4:
                            x[h][j] = x[h][j] - (n0 * u0 + n1 * u1) * over
                        else:
                            x[h][j] = x[h][j] - (m0 * u0 + m1 * u1)
                if h == g:
                    m0 = jnp.where(row == k1, pb * over_a, m0)
                top[h] = top[h] - (m0 * top_k[0] + m1 * top_k[1])
                inv[h] = inv[h] - (m0 * inv_k[0] + m1 * inv_k[1])
        roots = [lax.rsqrt(scale[h]) for h in range(2)]
        r = [top[h] * roots[h] for h in range(2)]
        w = [inv[h] * roots[h] for h in range(2)]
        q[p], q[p + 1] = w
        if p + 2 == panels:
            continue
        rt = jnp.concatenate(r, axis=0).T
        rk = [across_rows(r[k // ROWS], k % ROWS) for k in range(leaf)]
        wk = [across_rows(w[k // ROWS], k % ROWS) for k in range(leaf)]
        for i in range(p + 2, panels):
            parts = [rt[h * m + ROWS * i : h * m + ROWS * (i + 1)] for h in range(2)]
            coefs = [
                jnp.where(left, across_lanes(parts[0], k), across_lanes(parts[1], k))
                for k in range(leaf)
            ]
            sums = [None, None]
            for k in range(0, leaf, 2):
                for index, held in enumerate((rk, wk)):
                    both = coefs[k] * held[k] + coefs[k + 1] * held[k + 1]
                    sums[index] = both if sums[index] is None else sums[index] + both
            s[i] = s[i] - sums[0]
            q[i] = q[i] - sums[1]
    return jnp.concatenate(q, axis=0)


def inverse_factors(mats):
    m = mats[0].shape[0] // 2
    w11 = packed_factors(jnp.concatenate([s[:m, :m] for s in mats], axis=1))
    w11 = [w11[:, :m], w11[:, m:]]
    r12 = [mul(w, s[:m, m:]) for w, s in zip(w11, mats)]
    w22 = packed_factors(
        jnp.concatenate([s[m:, m:] - mul_tn(r, r) for r, s in zip(r12, mats)], axis=1)
    )
    w22 = [w22[:, :m], w22[:, m:]]
    w21 = [-mul(w, mul_tn(r, v)) for w, r, v in zip(w22, r12, w11)]
    zero = jnp.zeros((m, m), jnp.float32)
    return [
        jnp.concatenate(
            [jnp.concatenate([a, zero], axis=1), jnp.concatenate([b, c], axis=1)], axis=0
        )
        for a, b, c in zip(w11, w21, w22)
    ]


def window_kernel(
    slots_ref,
    masks_ref,
    coords_ref,
    fields_ref,
    white_ref,
    product_ref,
    coords_win,
    fields_win,
    s_ref,
    w_ref,
    xc_ref,
    mine_ref,
    other_ref,
    v_ref,
    terms_ref,
    back_ref,
    coords_send,
    coords_recv,
    fields_send,
    fields_recv,
    swap_send,
    swap_recv,
    back_send,
    back_recv,
):
    half, n = mine_ref.shape[0], mine_ref.shape[1]
    width = mine_ref.shape[2] // n
    per = fields_ref.shape[0]
    both = range(half)
    blk, grp, fld = (lax.axis_index(a) for a in ("blk", "grp", "fld"))
    blks, grps = lax.axis_size("blk"), lax.axis_size("grp")
    first = fld * half
    partner = {"fld": 1 - fld}
    routes = [(z, x) for z in (2, 1, 0) for x in (-1, 0, 1) if (z, x) != (0, 0)]

    def there(z, x):
        return (blk + z >= 0) & (blk + z < blks) & (grp + x >= 0) & (grp + x < grps)

    def place(z, x):
        return {"blk": blk + z, "grp": grp + x}

    coords_win[...] = jnp.zeros_like(coords_win)
    fields_win[...] = jnp.zeros_like(fields_win)
    barrier = pltpu.get_barrier_semaphore()
    pl.semaphore_signal(barrier, inc=1, device_id=partner, device_id_type=pl.DeviceIdType.MESH)
    around = jnp.int32(1)
    for z in range(-2, 3):
        for x in (-1, 0, 1):
            if (z, x) == (0, 0):
                continue

            @pl.when(there(z, x))
            def _():
                pl.semaphore_signal(
                    barrier, inc=1, device_id=place(z, x), device_id_type=pl.DeviceIdType.MESH
                )

            around = around + there(z, x).astype(jnp.int32)
    pl.semaphore_wait(barrier, around)

    def out_copy(source, window, send, recv, z, x):
        index = routes.index((z, x))
        cell = (2 - z) * 3 + 1 - x
        return pltpu.make_async_remote_copy(
            src_ref=source,
            dst_ref=window.at[pl.ds(cell * per, per)],
            send_sem=send.at[index],
            recv_sem=recv.at[index],
            device_id=place(z, x),
            device_id_type=pl.DeviceIdType.MESH,
        )

    def coords_copy(z, x):
        return out_copy(coords_ref, coords_win, coords_send, coords_recv, z, x)

    def fields_copy(z, x):
        return out_copy(fields_ref, fields_win, fields_send, fields_recv, z, x)

    def back_copy(z, x):
        index = routes.index((z, x))
        cell = (2 - z) * 3 + 1 - x
        return pltpu.make_async_remote_copy(
            src_ref=terms_ref.at[pl.ds(cell * per, per)],
            dst_ref=back_ref.at[index],
            send_sem=back_send.at[index],
            recv_sem=back_recv.at[index],
            device_id=place(-z, -x),
            device_id_type=pl.DeviceIdType.MESH,
        )

    def on(condition, act):
        @pl.when(condition)
        def _():
            act()

    for z, x in routes:
        on(there(z, x), lambda: coords_copy(z, x).start())
    for z, x in routes:
        on(there(z, x), lambda: fields_copy(z, x).start())
    own = (2 * 3 + 1) * per
    coords_win[pl.ds(own, per)] = coords_ref[...]
    fields_win[pl.ds(own, per)] = fields_ref[...]
    for z, x in routes:
        on(there(-z, -x), lambda: coords_copy(z, x).wait_recv())

    def slot(block, t):
        return slots_ref[block, t]

    for c in both:
        for t in range(width):
            pts = coords_win[slot(first + c, t)]
            for d in range(2):
                xc_ref[c, t, d] = jnp.broadcast_to(pts[d : d + 1], (n, n)).T
    eye = lax.broadcasted_iota(jnp.int32, (n, n), 0) == lax.broadcasted_iota(
        jnp.int32, (n, n), 1
    )
    factor = 3.0 / (ELL * ELL)
    for c in both:
        for u in range(width):
            pts = coords_win[slot(first + c, u)]
            mu = masks_ref[first + c, u]
            for t in range(u + 1):
                dx = xc_ref[c, t, 0] - pts[0:1]
                dy = xc_ref[c, t, 1] - pts[1:2]
                r2 = (dx * dx + dy * dy) * factor
                scaled = r2 * lax.rsqrt(jnp.maximum(r2, 1e-30))
                value = (1.0 + scaled) * jnp.exp(-scaled)
                value = value * (masks_ref[first + c, t] * mu)
                if t == u:
                    value = value + jnp.where(eye, NUGGET * mu + 1.0 - mu, 0.0)
                s_ref[c, t, :, u * n : (u + 1) * n] = value

    def step(t, carry):
        w = inverse_factors([s_ref[c, t, :, pl.ds(pl.multiple_of(t * n, n), n)] for c in both])
        for c in both:
            w_ref[c, t] = w[c]
        for tv in range(width - 1):

            @pl.when(t == tv)
            def _():
                b = [mul(w_ref[c, tv], s_ref[c, tv, :, (tv + 1) * n :]) for c in both]
                for c in both:
                    s_ref[c, tv, :, (tv + 1) * n :] = b[c]
                for u in range(tv + 1, width):
                    skip = (u - tv - 1) * n
                    for c in both:
                        s_ref[c, u, :, u * n :] = s_ref[c, u, :, u * n :] - mul_tn(
                            b[c][:, skip : skip + n], b[c][:, skip:]
                        )

        return carry

    lax.fori_loop(0, width, step, 0)

    def swap(t):
        piece = pl.ds(t * n, n)
        return pltpu.make_async_remote_copy(
            src_ref=mine_ref.at[:, :, piece],
            dst_ref=other_ref.at[:, :, piece],
            send_sem=swap_send.at[t],
            recv_sem=swap_recv.at[t],
            device_id=partner,
            device_id_type=pl.DeviceIdType.MESH,
        )

    for t in reversed(range(width)):
        for c in both:
            if t == width - 1:
                mine_ref[c, :, t * n :] = w_ref[c, t]
                continue
            later = (t + 1) * n
            total = mul_nt(mine_ref[c, :, later:], s_ref[c, t, :, later:])
            mine_ref[c, :, t * n : later] = -mul(total, w_ref[c, t])
        swap(t).start()
    for z, x in routes:
        on(there(-z, -x), lambda: fields_copy(z, x).wait_recv())

    def apply(source, start):
        for c in both:
            block = start + c
            values = jnp.concatenate([fields_win[slot(block, t)] for t in range(width)], axis=1)
            total = mul_nt(values, source[c])
            white_ref[block] = total
            v_ref[block] = mul(total, source[c])

    apply(mine_ref, first)
    for t in reversed(range(width)):
        swap(t).wait_recv()
    apply(other_ref, half - first)

    def gather_terms(z, x):
        cell = (2 - z) * 3 + 1 - x
        for i in range(per):
            total = None
            if (z, x) == (0, 0):
                total = v_ref[i, :, (width - 1) * n :]
            order = (2 - z) * per + i
            for block in range(per):
                if not block <= order < block + 2 * per:
                    continue
                for t in range(width - 1):
                    v = v_ref[block, :, t * n : (t + 1) * n]
                    part = jnp.where(slot(block, t) == cell * per + i, v, jnp.zeros_like(v))
                    total = part if total is None else total + part
            if total is None:
                total = jnp.zeros_like(terms_ref[0])
            terms_ref[cell * per + i] = total

    for z, x in routes:

        def send_terms(z=z, x=x):
            gather_terms(z, x)
            back_copy(z, x).start()

        on(there(-z, -x), send_terms)
    gather_terms(0, 0)
    product_ref[...] = terms_ref[pl.ds(own, per)]
    for index, (z, x) in enumerate(routes):

        def add_back(z=z, x=x, index=index):
            back_copy(z, x).wait_recv()
            product_ref[...] += back_ref[index]

        on(there(z, x), add_back)
    for t in range(width):
        swap(t).wait_send()
    for z, x in routes:

        def sent(z=z, x=x):
            coords_copy(z, x).wait_send()
            fields_copy(z, x).wait_send()

        on(there(z, x), sent)
        on(there(-z, -x), lambda: back_copy(z, x).wait_send())


def per_device(coords, fields, neighbours):
    per = coords.shape[0]
    local_fields = fields.shape[2]
    n = coords.shape[3]
    groups = lax.axis_size("grp")
    blk_pos = lax.axis_index("blk")
    grp_pos = lax.axis_index("grp")
    lists = neighbours.reshape(per, neighbours.shape[2])
    earlier = lists // groups - (blk_pos - 2) * per
    beside = lists % groups - grp_pos + 1
    listed = ((earlier // per) * 3 + beside) * per + earlier % per
    own_slot = (7 * per + jnp.arange(per, dtype=jnp.int32))[:, None]
    slots = jnp.concatenate([jnp.where(lists >= 0, listed, own_slot), own_slot], axis=1)
    masks = jnp.concatenate(
        [(lists >= 0).astype(jnp.float32), jnp.ones((per, 1), jnp.float32)], axis=1
    )
    width = slots.shape[1]
    half = per // lax.axis_size("fld")
    smem = pl.BlockSpec(memory_space=pltpu.SMEM)
    vmem = pl.BlockSpec(memory_space=pltpu.VMEM)
    block = (per, local_fields, n)
    dma = pltpu.SemaphoreType.DMA
    whitened, product = pl.pallas_call(
        window_kernel,
        out_shape=(jax.ShapeDtypeStruct(block, jnp.float32),) * 2,
        in_specs=[smem, smem, vmem, vmem],
        out_specs=(vmem, vmem),
        scratch_shapes=[
            pltpu.VMEM((9 * per, 2, n), jnp.float32),
            pltpu.VMEM((9 * per, local_fields, n), jnp.float32),
            pltpu.VMEM((half, width, n, width * n), jnp.float32),
            pltpu.VMEM((half, width, n, n), jnp.float32),
            pltpu.VMEM((half, width, 2, n, n), jnp.float32),
            pltpu.VMEM((half, n, width * n), jnp.float32),
            pltpu.VMEM((half, n, width * n), jnp.float32),
            pltpu.VMEM((per, local_fields, width * n), jnp.float32),
            pltpu.VMEM((9 * per, local_fields, n), jnp.float32),
            pltpu.VMEM((8,) + block, jnp.float32),
            dma((8,)),
            dma((8,)),
            dma((8,)),
            dma((8,)),
            dma((width,)),
            dma((width,)),
            dma((8,)),
            dma((8,)),
        ],
        compiler_params=pltpu.CompilerParams(
            vmem_limit_bytes=40 * 1024 * 1024, collective_id=0, has_side_effects=True
        ),
        name="window",
    )(slots, masks, coords.reshape(per, 2, n), fields.reshape(block))
    return (whitened[:, None], product[:, None])


def solution(mesh):
    return jax.shard_map(
        per_device,
        mesh=mesh,
        in_specs=(
            P(("parts", "blk"), "grp", None, None),
            P(("parts", "blk"), "grp", "fld", None),
            P(("parts", "blk"), "grp", None),
        ),
        out_specs=(
            P(("parts", "blk"), "grp", "fld", None),
            P(("parts", "blk"), "grp", "fld", None),
        ),
        check_vma=False,
    )
```

```python
import functools

import jax
import jax.numpy as jnp
from jax import lax
from jax.experimental import pallas as pl
from jax.experimental.pallas import tpu as pltpu
from jax.sharding import PartitionSpec as P

ELL = 0.3
NUGGET = 0.25
ROWS = 8
HIGHEST = lax.Precision.HIGHEST


def dot(a, b, dims):
    return lax.dot_general(
        a, b, (dims, ((), ())), precision=HIGHEST, preferred_element_type=jnp.float32
    )


def mul(a, b):
    return dot(a, b, ((1,), (0,)))


def mul_tn(a, b):
    return dot(a, b, ((0,), (0,)))


def mul_nt(a, b):
    return dot(a, b, ((1,), (1,)))


def across_lanes(x, lane):
    return jnp.broadcast_to(x[:, lane : lane + 1], x.shape[:1] + (128,))


def across_rows(x, row):
    return jnp.broadcast_to(x[row : row + 1, :], x.shape)


def packed_factors(pair):
    m, n = pair.shape
    panels = m // ROWS
    row = lax.broadcasted_iota(jnp.int32, (ROWS, n), 0)
    lane = lax.broadcasted_iota(jnp.int32, (ROWS, n), 1)
    left = lane < m
    s = [pair[ROWS * i : ROWS * (i + 1)] for i in range(panels)]
    q = [
        jnp.where(lane % m == row + ROWS * i, 1.0, 0.0).astype(jnp.float32) for i in range(panels)
    ]
    leaf = 2 * ROWS
    for p in range(0, panels, 2):
        top = [s[p], s[p + 1]]
        inv = [q[p], q[p + 1]]
        x = [
            [
                jnp.where(
                    left,
                    across_lanes(top[h], ROWS * p + j),
                    across_lanes(top[h], m + ROWS * p + j),
                )
                for j in range(leaf)
            ]
            for h in range(2)
        ]
        scale = [jnp.ones_like(top[0]) for _ in range(2)]
        for k in range(0, leaf, 2):
            g, k0 = k // ROWS, k % ROWS
            k1 = k0 + 1
            pa = across_rows(x[g][k], k0)
            pb = across_rows(x[g][k + 1], k0)
            pc = across_rows(x[g][k + 1], k1)
            det = pa * pc - pb * pb
            over = 1.0 / det
            over_a = 1.0 / pa
            scale[g] = jnp.where(row == k0, pa, jnp.where(row == k1, det * over_a, scale[g]))
            rows_j = {
                j: (across_rows(x[g][j], k0), across_rows(x[g][j], k1))
                for j in range(k + 2, leaf)
            }
            top_k = (across_rows(top[g], k0), across_rows(top[g], k1))
            inv_k = (across_rows(inv[g], k0), across_rows(inv[g], k1))
            for h in range(g, 2):
                n0 = pc * x[h][k] - pb * x[h][k + 1]
                n1 = pa * x[h][k + 1] - pb * x[h][k]
                if h == g:
                    n0 = jnp.where(row > k1, n0, 0.0)
                    n1 = jnp.where(row > k1, n1, 0.0)
                m0 = n0 * over
                m1 = n1 * over
                if not (h == g and k1 == ROWS - 1):
                    for j in range(k + 2, leaf):
                        u0, u1 = rows_j[j]
                        if j < k + 4:
                            x[h][j] = x[h][j] - (n0 * u0 + n1 * u1) * over
                        else:
                            x[h][j] = x[h][j] - (m0 * u0 + m1 * u1)
                if h == g:
                    m0 = jnp.where(row == k1, pb * over_a, m0)
                top[h] = top[h] - (m0 * top_k[0] + m1 * top_k[1])
                inv[h] = inv[h] - (m0 * inv_k[0] + m1 * inv_k[1])
        roots = [lax.rsqrt(scale[h]) for h in range(2)]
        r = [top[h] * roots[h] for h in range(2)]
        w = [inv[h] * roots[h] for h in range(2)]
        q[p], q[p + 1] = w
        if p + 2 == panels:
            continue
        rt = jnp.concatenate(r, axis=0).T
        rk = [across_rows(r[k // ROWS], k % ROWS) for k in range(leaf)]
        wk = [across_rows(w[k // ROWS], k % ROWS) for k in range(leaf)]
        for i in range(p + 2, panels):
            parts = [rt[h * m + ROWS * i : h * m + ROWS * (i + 1)] for h in range(2)]
            coefs = [
                jnp.where(left, across_lanes(parts[0], k), across_lanes(parts[1], k))
                for k in range(leaf)
            ]
            sums = [None, None]
            for k in range(0, leaf, 2):
                for index, held in enumerate((rk, wk)):
                    both = coefs[k] * held[k] + coefs[k + 1] * held[k + 1]
                    sums[index] = both if sums[index] is None else sums[index] + both
            s[i] = s[i] - sums[0]
            q[i] = q[i] - sums[1]
    return jnp.concatenate(q, axis=0)


def inverse_factors(mats):
    m = mats[0].shape[0] // 2
    w11 = packed_factors(jnp.concatenate([s[:m, :m] for s in mats], axis=1))
    w11 = [w11[:, :m], w11[:, m:]]
    r12 = [mul(w, s[:m, m:]) for w, s in zip(w11, mats)]
    w22 = packed_factors(
        jnp.concatenate([s[m:, m:] - mul_tn(r, r) for r, s in zip(r12, mats)], axis=1)
    )
    w22 = [w22[:, :m], w22[:, m:]]
    w21 = [-mul(w, mul_tn(r, v)) for w, r, v in zip(w22, r12, w11)]
    zero = jnp.zeros((m, m), jnp.float32)
    return [
        jnp.concatenate(
            [jnp.concatenate([a, zero], axis=1), jnp.concatenate([b, c], axis=1)], axis=0
        )
        for a, b, c in zip(w11, w21, w22)
    ]


def window_kernel(
    slots_ref,
    masks_ref,
    coords_ref,
    fields_ref,
    white_ref,
    product_ref,
    coords_win,
    fields_win,
    s_ref,
    w_ref,
    xc_ref,
    mine_ref,
    other_ref,
    v_ref,
    terms_ref,
    back_ref,
    coords_send,
    coords_recv,
    fields_send,
    fields_recv,
    swap_send,
    swap_recv,
    back_send,
    back_recv,
):
    half, n = mine_ref.shape[0], mine_ref.shape[1]
    width = mine_ref.shape[2] // n
    per = fields_ref.shape[0]
    both = range(half)
    blk, grp, fld = (lax.axis_index(a) for a in ("blk", "grp", "fld"))
    blks, grps = lax.axis_size("blk"), lax.axis_size("grp")
    first = fld * half
    partner = {"fld": 1 - fld}
    routes = [(z, x) for z in (2, 1, 0) for x in (-1, 0, 1) if (z, x) != (0, 0)]

    def there(z, x):
        return (blk + z >= 0) & (blk + z < blks) & (grp + x >= 0) & (grp + x < grps)

    def place(z, x):
        return {"blk": blk + z, "grp": grp + x}

    coords_win[...] = jnp.zeros_like(coords_win)
    fields_win[...] = jnp.zeros_like(fields_win)
    barrier = pltpu.get_barrier_semaphore()
    pl.semaphore_signal(barrier, inc=1, device_id=partner, device_id_type=pl.DeviceIdType.MESH)
    around = jnp.int32(1)
    for z in range(-2, 3):
        for x in (-1, 0, 1):
            if (z, x) == (0, 0):
                continue

            @pl.when(there(z, x))
            def _():
                pl.semaphore_signal(
                    barrier, inc=1, device_id=place(z, x), device_id_type=pl.DeviceIdType.MESH
                )

            around = around + there(z, x).astype(jnp.int32)
    pl.semaphore_wait(barrier, around)

    def out_copy(source, window, send, recv, z, x):
        index = routes.index((z, x))
        cell = (2 - z) * 3 + 1 - x
        return pltpu.make_async_remote_copy(
            src_ref=source,
            dst_ref=window.at[pl.ds(cell * per, per)],
            send_sem=send.at[index],
            recv_sem=recv.at[index],
            device_id=place(z, x),
            device_id_type=pl.DeviceIdType.MESH,
        )

    def coords_copy(z, x):
        return out_copy(coords_ref, coords_win, coords_send, coords_recv, z, x)

    def fields_copy(z, x):
        return out_copy(fields_ref, fields_win, fields_send, fields_recv, z, x)

    def back_copy(z, x):
        index = routes.index((z, x))
        cell = (2 - z) * 3 + 1 - x
        return pltpu.make_async_remote_copy(
            src_ref=terms_ref.at[pl.ds(cell * per, per)],
            dst_ref=back_ref.at[index],
            send_sem=back_send.at[index],
            recv_sem=back_recv.at[index],
            device_id=place(-z, -x),
            device_id_type=pl.DeviceIdType.MESH,
        )

    def on(condition, act):
        @pl.when(condition)
        def _():
            act()

    for z, x in routes:
        on(there(z, x), lambda: coords_copy(z, x).start())
    for z, x in routes:
        on(there(z, x), lambda: fields_copy(z, x).start())
    own = (2 * 3 + 1) * per
    coords_win[pl.ds(own, per)] = coords_ref[...]
    fields_win[pl.ds(own, per)] = fields_ref[...]
    for z, x in routes:
        on(there(-z, -x), lambda: coords_copy(z, x).wait_recv())

    def slot(block, t):
        return slots_ref[block, t]

    for c in both:
        for t in range(width):
            pts = coords_win[slot(first + c, t)]
            for d in range(2):
                xc_ref[c, t, d] = jnp.broadcast_to(pts[d : d + 1], (n, n)).T
    eye = lax.broadcasted_iota(jnp.int32, (n, n), 0) == lax.broadcasted_iota(
        jnp.int32, (n, n), 1
    )
    factor = 3.0 / (ELL * ELL)
    for c in both:
        for u in range(width):
            pts = coords_win[slot(first + c, u)]
            mu = masks_ref[first + c, u]
            for t in range(u + 1):
                dx = xc_ref[c, t, 0] - pts[0:1]
                dy = xc_ref[c, t, 1] - pts[1:2]
                r2 = (dx * dx + dy * dy) * factor
                scaled = r2 * lax.rsqrt(jnp.maximum(r2, 1e-30))
                value = (1.0 + scaled) * jnp.exp(-scaled)
                value = value * (masks_ref[first + c, t] * mu)
                if t == u:
                    value = value + jnp.where(eye, NUGGET * mu + 1.0 - mu, 0.0)
                s_ref[c, t, :, u * n : (u + 1) * n] = value

    diagonal = [s_ref[c, 0, :, :n] for c in both]
    for t in range(width):
        w = inverse_factors(diagonal)
        for c in both:
            w_ref[c, t] = w[c]
        if t + 1 == width:
            break
        near = slice((t + 1) * n, (t + 2) * n)
        far = slice((t + 2) * n, width * n)
        b = [mul(w[c], s_ref[c, t, :, near]) for c in both]
        diagonal = [s_ref[c, t + 1, :, near] - mul_tn(b[c], b[c]) for c in both]
        for c in both:
            s_ref[c, t, :, near] = b[c]
            if t + 2 == width:
                continue
            rest = mul(w[c], s_ref[c, t, :, far])
            s_ref[c, t, :, far] = rest
            s_ref[c, t + 1, :, far] = s_ref[c, t + 1, :, far] - mul_tn(b[c], rest)
            for u in range(t + 2, width):
                skip = (u - t - 2) * n
                s_ref[c, u, :, u * n :] = s_ref[c, u, :, u * n :] - mul_tn(
                    rest[:, skip : skip + n], rest[:, skip:]
                )

    def swap(t):
        piece = pl.ds(t * n, n)
        return pltpu.make_async_remote_copy(
            src_ref=mine_ref.at[:, :, piece],
            dst_ref=other_ref.at[:, :, piece],
            send_sem=swap_send.at[t],
            recv_sem=swap_recv.at[t],
            device_id=partner,
            device_id_type=pl.DeviceIdType.MESH,
        )

    for t in reversed(range(width)):
        for c in both:
            if t == width - 1:
                mine_ref[c, :, t * n :] = w_ref[c, t]
                continue
            later = (t + 1) * n
            total = mul_nt(mine_ref[c, :, later:], s_ref[c, t, :, later:])
            mine_ref[c, :, t * n : later] = -mul(total, w_ref[c, t])
        swap(t).start()
    for z, x in routes:
        on(there(-z, -x), lambda: fields_copy(z, x).wait_recv())

    def apply(source, start):
        for c in both:
            block = start + c
            values = jnp.concatenate([fields_win[slot(block, t)] for t in range(width)], axis=1)
            total = mul_nt(values, source[c])
            white_ref[block] = total
            v_ref[block] = mul(total, source[c])

    apply(mine_ref, first)
    for t in reversed(range(width)):
        swap(t).wait_recv()
    apply(other_ref, half - first)

    def gather_terms(z, x):
        cell = (2 - z) * 3 + 1 - x
        for i in range(per):
            total = None
            if (z, x) == (0, 0):
                total = v_ref[i, :, (width - 1) * n :]
            order = (2 - z) * per + i
            for block in range(per):
                if not block <= order < block + 2 * per:
                    continue
                for t in range(width - 1):
                    v = v_ref[block, :, t * n : (t + 1) * n]
                    part = jnp.where(slot(block, t) == cell * per + i, v, jnp.zeros_like(v))
                    total = part if total is None else total + part
            if total is None:
                total = jnp.zeros_like(terms_ref[0])
            terms_ref[cell * per + i] = total

    for z, x in routes:

        def send_terms(z=z, x=x):
            gather_terms(z, x)
            back_copy(z, x).start()

        on(there(-z, -x), send_terms)
    gather_terms(0, 0)
    product_ref[...] = terms_ref[pl.ds(own, per)]
    for index, (z, x) in enumerate(routes):

        def add_back(z=z, x=x, index=index):
            back_copy(z, x).wait_recv()
            product_ref[...] += back_ref[index]

        on(there(z, x), add_back)
    for t in range(width):
        swap(t).wait_send()
    for z, x in routes:

        def sent(z=z, x=x):
            coords_copy(z, x).wait_send()
            fields_copy(z, x).wait_send()

        on(there(z, x), sent)
        on(there(-z, -x), lambda: back_copy(z, x).wait_send())


def per_device(coords, fields, neighbours):
    per = coords.shape[0]
    local_fields = fields.shape[2]
    n = coords.shape[3]
    groups = lax.axis_size("grp")
    blk_pos = lax.axis_index("blk")
    grp_pos = lax.axis_index("grp")
    lists = neighbours.reshape(per, neighbours.shape[2])
    earlier = lists // groups - (blk_pos - 2) * per
    beside = lists % groups - grp_pos + 1
    listed = ((earlier // per) * 3 + beside) * per + earlier % per
    own_slot = (7 * per + jnp.arange(per, dtype=jnp.int32))[:, None]
    slots = jnp.concatenate([jnp.where(lists >= 0, listed, own_slot), own_slot], axis=1)
    masks = jnp.concatenate(
        [(lists >= 0).astype(jnp.float32), jnp.ones((per, 1), jnp.float32)], axis=1
    )
    width = slots.shape[1]
    half = per // lax.axis_size("fld")
    smem = pl.BlockSpec(memory_space=pltpu.SMEM)
    vmem = pl.BlockSpec(memory_space=pltpu.VMEM)
    block = (per, local_fields, n)
    dma = pltpu.SemaphoreType.DMA
    whitened, product = pl.pallas_call(
        window_kernel,
        out_shape=(jax.ShapeDtypeStruct(block, jnp.float32),) * 2,
        in_specs=[smem, smem, vmem, vmem],
        out_specs=(vmem, vmem),
        scratch_shapes=[
            pltpu.VMEM((9 * per, 2, n), jnp.float32),
            pltpu.VMEM((9 * per, local_fields, n), jnp.float32),
            pltpu.VMEM((half, width, n, width * n), jnp.float32),
            pltpu.VMEM((half, width, n, n), jnp.float32),
            pltpu.VMEM((half, width, 2, n, n), jnp.float32),
            pltpu.VMEM((half, n, width * n), jnp.float32),
            pltpu.VMEM((half, n, width * n), jnp.float32),
            pltpu.VMEM((per, local_fields, width * n), jnp.float32),
            pltpu.VMEM((9 * per, local_fields, n), jnp.float32),
            pltpu.VMEM((8,) + block, jnp.float32),
            dma((8,)),
            dma((8,)),
            dma((8,)),
            dma((8,)),
            dma((width,)),
            dma((width,)),
            dma((8,)),
            dma((8,)),
        ],
        compiler_params=pltpu.CompilerParams(
            vmem_limit_bytes=40 * 1024 * 1024, collective_id=0, has_side_effects=True
        ),
        name="window",
    )(slots, masks, coords.reshape(per, 2, n), fields.reshape(block))
    return (whitened[:, None], product[:, None])


def solution(mesh):
    return jax.shard_map(
        per_device,
        mesh=mesh,
        in_specs=(
            P(("parts", "blk"), "grp", None, None),
            P(("parts", "blk"), "grp", "fld", None),
            P(("parts", "blk"), "grp", None),
        ),
        out_specs=(
            P(("parts", "blk"), "grp", "fld", None),
            P(("parts", "blk"), "grp", "fld", None),
        ),
        check_vma=False,
    )
```
